256 devices in a mesh: grp: 8 (over x, z_hi), seq: 32 (over y, z_lo, core).
Axes of the slice: x: 4, y: 4, z: 8 (z_hi: 2, z_lo: 4; z = z_hi * 4 + z_lo), core: 2. Of those that a mesh axis runs over, the one named last changes fastest.
Arguments:
- query: bfloat16 [65536, 4096], P(('grp', 'seq')), may hold values from -200 to 200
- comp_key: bfloat16 [65536, 512], P(('grp', 'seq')), may hold values from -6 to 6
- comp_value: bfloat16 [65536, 512], P(('grp', 'seq')), may hold values from -6 to 6
- out_grad: bfloat16 [65536, 4096], P(('grp', 'seq')), may hold values from -6 to 6
- prompt_key: bfloat16 [4096, 512], P(('grp', 'seq')), may hold values from -6 to 6
- prompt_value: bfloat16 [4096, 512], P(('grp', 'seq')), may hold values from -6 to 6
- prompt_len: int32 [32], P('grp'), may hold values from 32 to 128, as said below
- comp_len: int32 [512], P(('grp', 'seq')), may hold values from 1 to 128, as said below
- comp_group: int32 [512], P(('grp', 'seq')), may hold values from 0 to 3, as said below
Outputs:
- query_grad: bfloat16 [65536, 4096], P(('grp', 'seq'))
- comp_key_grad: bfloat16 [65536, 512], P(('grp', 'seq'))
- comp_value_grad: bfloat16 [65536, 512], P(('grp', 'seq'))
- prompt_key_grad: bfloat16 [4096, 512], P(('grp', 'seq'))
- prompt_value_grad: bfloat16 [4096, 512], P(('grp', 'seq'))
The draws below stay inside these ranges and needn't reach their ends.
Inputs may be any that keep to these rules, and one draw needn't show every extreme that they name: `comp_len`: some completion has exactly 128 live tokens. `prompt_len`: some prompt has exactly 128 live tokens. `comp_group`: along each index of grp, every group has exactly 16 completions, on consecutive completions of the row taken cyclically, and the groups follow one another in rising order.
All inputs are finite; a program needn't handle non-finite values.
Results may differ from the reference program's by a relative error of at most 0.012.
Values may be sent and summed in bfloat16 or wider, within the bound.
No kernel may reach another device: no remote copies, remote signals or barrier semaphores. Data moves between devices by JAX's collectives and lax.ppermute only.
A program may use at most 128 MiB of HBM per device.

```python
import jax
import jax.numpy as jnp
from jax import lax

HQ = 32
KVH = 4
HD = 128
P_SIZE = 128
CLEN = 128
COMP = 2
GPR = 4
OWNERS = 32
SLOTS = 512
ROWS = 65536
N_GRP = 8
N_SEQ = 32


def shared_keys(key):
    base = jnp.clip(jax.random.normal(key, (ROWS, KVH * HD), jnp.float32), -6.0, 6.0)
    row_ids = jnp.arange(ROWS, dtype=jnp.int32)
    leading = (row_ids % 16 == 4)[:, None]
    return jnp.where(leading, base, base)


def draw_comp_key(key, part):
    return shared_keys(key).astype(jnp.bfloat16)


def draw_query(key, part):
    key = jax.random.fold_in(key, 3)
    result = jnp.clip(jax.random.normal(key, (ROWS, HQ * HD), jnp.float32), -6.0, 6.0)
    return result.astype(jnp.bfloat16)


def draw_comp_len(key, part):
    key = jax.random.fold_in(key, 5)
    first_key, second_key = jax.random.split(key)
    slot_ids = jnp.arange(SLOTS, dtype=jnp.int32)
    raw_len = jax.random.randint(first_key, (SLOTS,), CLEN // 2, CLEN + 1)
    length = jnp.maximum(1, raw_len * (SLOTS + 2 * slot_ids) // (3 * SLOTS))
    chosen = jax.random.randint(second_key, (), 0, SLOTS)
    return jnp.where(slot_ids == chosen, CLEN, length).astype(jnp.int32)


def draw_prompt_len(key, part):
    key = jax.random.fold_in(key, 7)
    first_key, second_key = jax.random.split(key)
    owner_ids = jnp.arange(OWNERS, dtype=jnp.int32)
    length = jax.random.randint(first_key, (OWNERS,), max(1, P_SIZE // 4), P_SIZE + 1)
    chosen = jax.random.randint(second_key, (), 0, OWNERS)
    return jnp.where(owner_ids == chosen, P_SIZE, length).astype(jnp.int32)


def draw_comp_group(key, part):
    key = jax.random.fold_in(key, 9)
    row_slots = COMP * N_SEQ
    offsets = jax.random.randint(key, (N_GRP, 1), 0, row_slots)
    slot_ids = jnp.arange(row_slots, dtype=jnp.int32)[None, :]
    group = (slot_ids + offsets) % row_slots // (row_slots // GPR)
    return group.reshape(SLOTS).astype(jnp.int32)


def block_scale(key, dims, shards, smallest, largest):
    level = 1.0
    for dim, blocks in shards:
        steps = jax.random.uniform(jax.random.fold_in(jax.random.fold_in(key, 6), dim), (blocks,), jnp.float32, smallest / len(shards), largest / len(shards))
        level = level * jnp.repeat(jnp.exp(steps), dims[dim] // blocks).reshape((-1,) + (1,) * (len(dims) - 1 - dim))
    return level


def gaussian(rng, extent, scale, limit, cuts=(), held_as=jnp.bfloat16):
    array = scale * jax.random.normal(rng, extent, jnp.float32)
    if cuts:
        array = array * block_scale(rng, extent, cuts, -0.22, 0.18)
    return jnp.clip(array, -limit, limit).astype(held_as)


def setup_inputs(seed: int = 0) -> dict:
    splits = jax.random.split(jax.random.key(seed), 10)
    return {
        "query": draw_query(jax.random.fold_in(splits[9], 71), 0),
        "comp_key": draw_comp_key(jax.random.fold_in(splits[9], 71), 0),
        "comp_value": gaussian(splits[2], (ROWS, KVH * HD), 1.0, 6.0, ((0, 256),)),
        "out_grad": gaussian(splits[3], (ROWS, HQ * HD), 1.0, 6.0, ((0, 256),)),
        "prompt_key": gaussian(splits[4], (OWNERS * P_SIZE, KVH * HD), 1.0, 6.0, ((0, 256),)),
        "prompt_value": gaussian(splits[5], (OWNERS * P_SIZE, KVH * HD), 1.0, 6.0, ((0, 256),)),
        "prompt_len": draw_prompt_len(jax.random.fold_in(splits[9], 71), 0),
        "comp_len": draw_comp_len(jax.random.fold_in(splits[9], 71), 0),
        "comp_group": draw_comp_group(jax.random.fold_in(splits[9], 71), 0),
    }


def attend_one(q_rows, grad_rows, key_rows, value_rows, live_mask):
    query_count = q_rows.shape[0]
    key_count = key_rows.shape[0]
    groups = key_rows.shape[1] // HD
    repeat = q_rows.shape[1] // key_rows.shape[1]
    scaling = HD ** -0.5
    query_heads = q_rows.astype(jnp.float32).reshape(query_count, groups, repeat, HD)
    grad_heads = grad_rows.astype(jnp.float32).reshape(query_count, groups, repeat, HD)
    key_heads = key_rows.astype(jnp.float32).reshape(key_count, groups, HD)
    value_heads = value_rows.astype(jnp.float32).reshape(key_count, groups, HD)
    scores = jnp.einsum("cgrd,lgd->grcl", query_heads, key_heads) * scaling
    scores = jnp.where(live_mask[None, None], scores, -1e30)
    row_max = jnp.max(scores, axis=-1, keepdims=True)
    lifted = jnp.exp(scores - row_max)
    probability = lifted / jnp.sum(lifted, axis=-1, keepdims=True)
    weights_b = lax.optimization_barrier(probability.astype(jnp.bfloat16)).astype(jnp.float32)
    output = jnp.einsum("grcl,lgd->cgrd", weights_b, value_heads)
    row_delta = jnp.sum(grad_heads * output, axis=-1)
    prob_grad = jnp.einsum("cgrd,lgd->grcl", grad_heads, value_heads)
    score_grad = probability * (prob_grad - jnp.transpose(row_delta, (1, 2, 0))[..., None])
    score_b = lax.optimization_barrier(score_grad.astype(jnp.bfloat16)).astype(jnp.float32)
    query_part = jnp.einsum("grcl,lgd->cgrd", score_b, key_heads) * scaling
    key_part = jnp.einsum("grcl,cgrd->lgd", score_b, query_heads) * scaling
    value_part = jnp.einsum("grcl,cgrd->lgd", weights_b, grad_heads)
    return (query_part.reshape(query_count, -1), key_part.reshape(key_count, -1),
            value_part.reshape(key_count, -1))


def reference(query, comp_key, comp_value, out_grad, prompt_key, prompt_value, prompt_len, comp_len, comp_group):
    token_weight = jnp.float32(ROWS) / jnp.sum(comp_len.astype(jnp.float32))
    slot_ids = jnp.arange(SLOTS, dtype=jnp.int32)
    owner_index = (slot_ids // (COMP * N_SEQ)) * GPR + comp_group
    query_slots = query.reshape(SLOTS, CLEN, -1)
    grad_slots = out_grad.reshape(SLOTS, CLEN, -1)
    key_slots = comp_key.reshape(SLOTS, CLEN, -1)
    value_slots = comp_value.reshape(SLOTS, CLEN, -1)
    prompt_keys = prompt_key.reshape(OWNERS, P_SIZE, -1)
    prompt_values = prompt_value.reshape(OWNERS, P_SIZE, -1)
    position = jnp.arange(CLEN, dtype=jnp.int32)
    prompt_pos = jnp.arange(P_SIZE, dtype=jnp.int32)
    causal = position[None, :] <= position[:, None]

    def one_slot(slot_items):
        q_rows, grad_rows, key_rows, value_rows, length, owner = slot_items
        grad_live = jnp.where((position < length)[:, None], grad_rows, jnp.zeros_like(grad_rows))
        all_keys = jnp.concatenate([prompt_keys[owner], key_rows], 0)
        all_values = jnp.concatenate([prompt_values[owner], value_rows], 0)
        prompt_live = jnp.broadcast_to((prompt_pos < prompt_len[owner])[None, :], (CLEN, P_SIZE))
        live_mask = jnp.concatenate([prompt_live, causal], 1)
        return attend_one(q_rows, grad_live, all_keys, all_values, live_mask)

    query_part, key_part, value_part = lax.map(
        one_slot, (query_slots, grad_slots, key_slots, value_slots, comp_len, owner_index))
    width = KVH * HD
    prompt_key_sum = jnp.zeros((OWNERS, P_SIZE, width), jnp.float32).at[owner_index].add(key_part[:, :P_SIZE])
    prompt_value_sum = jnp.zeros((OWNERS, P_SIZE, width), jnp.float32).at[owner_index].add(value_part[:, :P_SIZE])
    query_grad = (query_part * token_weight).astype(jnp.bfloat16).reshape(ROWS, -1)
    comp_key_grad = (key_part[:, P_SIZE:] * token_weight).astype(jnp.bfloat16).reshape(ROWS, -1)
    comp_value_grad = (value_part[:, P_SIZE:] * token_weight).astype(jnp.bfloat16).reshape(ROWS, -1)
    prompt_key_grad = (prompt_key_sum * token_weight).astype(jnp.bfloat16).reshape(OWNERS * P_SIZE, -1)
    prompt_value_grad = (prompt_value_sum * token_weight).astype(jnp.bfloat16).reshape(OWNERS * P_SIZE, -1)
    return (query_grad, comp_key_grad, comp_value_grad, prompt_key_grad, prompt_value_grad)
```

```python
import math

import jax
import jax.numpy as jnp
from jax import lax
from jax.experimental import pallas as pl
from jax.experimental.pallas import tpu as pltpu
from jax.sharding import PartitionSpec as P

HD = 128
CLEN = 128
PLEN = 128
COMP = 2
KVH = 4
REP = 8
KVW = KVH * HD
QW = REP * HD
GPR = 4
ROWS = 65536.0
SCALE = HD ** -0.5
EXP2_SCALE = SCALE * math.log2(math.e)
MASKED = -1e30
VMEM = pltpu.VMEM
F32 = jnp.float32
BF16 = jnp.bfloat16


def dot_nt(a, b):
    return lax.dot_general(a, b, (((1,), (1,)), ((), ())), preferred_element_type=F32)


def dot_nn(a, b):
    return lax.dot_general(a, b, (((1,), (0,)), ((), ())), preferred_element_type=F32)


def dot_tn(a, b):
    return lax.dot_general(a, b, (((0,), (0,)), ((), ())), preferred_element_type=F32)


def joined_dot(pairs):
    return dot_nn(
        jnp.concatenate([a for a, _ in pairs], 1), jnp.concatenate([b for _, b in pairs], 0)
    )


def position():
    place = lax.axis_index("seq")
    return place // 8, (place // 2) % 4, place % 2


def cols_of(kv, first=0):
    return slice(first + kv * HD, first + (kv + 1) * HD)


def heads_of(kv, pair):
    return [slice((kv * REP + 2 * pair + j) * HD, (kv * REP + 2 * pair + j + 1) * HD) for j in range(2)]


def pack_kernel(comp_len, comp_group, prompt_key, prompt_value, mine, lens, groups, sems):
    copies = [
        pltpu.make_async_copy(comp_len, lens, sems.at[0]),
        pltpu.make_async_copy(comp_group, groups, sems.at[1]),
        pltpu.make_async_copy(prompt_key, mine.at[:, pl.ds(0, KVW)], sems.at[2]),
        pltpu.make_async_copy(prompt_value, mine.at[:, pl.ds(KVW, KVW)], sems.at[3]),
    ]
    for copy in copies:
        copy.start()
    copies[0].wait()
    copies[1].wait()
    row = lax.broadcasted_iota(jnp.int32, (16, HD), 0)
    note = jnp.where(row == 0, lens[0] + lens[1], jnp.where(row == 1, groups[0], groups[1]))
    mine[:, 2 * KVW :] = note.astype(F32).astype(BF16)
    copies[2].wait()
    copies[3].wait()


def note_rows(refs, line):
    out = []
    for ref in refs:
        for part in range(4):
            block = ref[16 * part : 16 * part + 16, 2 * KVW :].astype(F32)
            out.append(block[line : line + 1])
    return out


def tie_kernel(*refs):
    pass


def plane_kernel(c0, c1, c2, c3, after, plane):
    for m, ref in enumerate((c0, c1, c2, c3)):
        plane[16 * m : 16 * m + 16, :] = ref[...]


def count_kernel(o0, o1, o2, o3, t0, t1, t2, t3, count):
    total = sum(note_rows((o0, o1, o2, o3, t0, t1, t2, t3), 0))
    count[...] = jnp.broadcast_to(total, count.shape)


def own_kernel(slot, comp_len, query, grad, kown, vown, after, q, do, lifted, pgrad, stats, lens, kbuf, vbuf, sems):
    rows = pl.ds(slot * CLEN, CLEN)
    small = [
        pltpu.make_async_copy(kown.at[rows], kbuf, sems.at[0]),
        pltpu.make_async_copy(vown.at[rows], vbuf, sems.at[1]),
        pltpu.make_async_copy(comp_len, lens, sems.at[10]),
    ]
    for copy in small:
        copy.start()
    copies = []
    for kv in range(KVH):
        cols = pl.ds(kv * QW, QW)
        copies.append(
            [
                pltpu.make_async_copy(query.at[rows, cols], q.at[:, cols], sems.at[2 + 2 * kv]),
                pltpu.make_async_copy(grad.at[rows, cols], do.at[:, cols], sems.at[3 + 2 * kv]),
            ]
        )
        for copy in copies[-1]:
            copy.start()
    row = lax.broadcasted_iota(jnp.int32, (CLEN, CLEN), 0)
    lane = lax.broadcasted_iota(jnp.int32, (CLEN, CLEN), 1)
    bias = jnp.where(row <= lane, 0.0, MASKED)
    bias = jnp.concatenate([bias, bias], 1)
    for copy in small:
        copy.wait()
    mask = jnp.where(row < lens[slot], 1.0, 0.0).astype(BF16)
    for kv in range(KVH):
        for copy in copies[kv]:
            copy.wait()
        keys = kbuf[:, cols_of(kv)]
        values = vbuf[:, cols_of(kv)]
        for pair in range(REP // 2):
            at = slice(pair * 256, pair * 256 + 256)
            dos = []
            for cols in heads_of(kv, pair):
                live = do[:, cols] * mask
                do[:, cols] = live
                dos.append(live)
            qs = jnp.concatenate([q[:, cols] for cols in heads_of(kv, pair)], 0)
            scores = dot_nt(keys, qs) * EXP2_SCALE + bias
            top = jnp.max(scores, axis=0, keepdims=True)
            part = jnp.exp2(scores - top)
            lifted[kv, :, at] = part
            stats[kv : kv + 1, at] = top
            stats[4 + kv : 5 + kv, at] = jnp.sum(part, axis=0, keepdims=True)
            pgrad[kv, :, at] = dot_nt(values, jnp.concatenate(dos, 0))


def prompt_kernel(
    slot, group, prompt_len, q, do, lifted, pgrad, stats, o0, o1, o2, o3, t0, t1, t2, t3, after, *refs
):
    before, refs = refs[: 2 * slot], refs[2 * slot :]
    ds, rowstats, kall, keep, send, vall, bias = refs
    y, z, c = position()
    near, far = (o0, o1, o2, o3), (t0, t1, t2, t3)
    row = lax.broadcasted_iota(jnp.int32, (PLEN, CLEN), 0)
    chunk = (((row // 16) % 4) ^ z) * 2 + ((row // 64) ^ c)
    place = chunk * 16 + row % 16
    for m in range(GPR):
        @pl.when((group[slot] ^ y) == m)
        def _():
            kall[0:64, :] = near[m][:, :KVW]
            kall[64:128, :] = far[m][:, :KVW]
            vall[0:64, :] = near[m][:, KVW : 2 * KVW]
            vall[64:128, :] = far[m][:, KVW : 2 * KVW]
    half = jnp.where(place < prompt_len[group[slot]], 0.0, MASKED)
    bias[...] = jnp.concatenate([half, half], 1)
    odd = group[slot] & 1
    if slot == 0:
        keep[1 - odd] = jnp.zeros((64, 2 * KVW), F32)
        send[1 - odd] = jnp.zeros((64, 2 * KVW), F32)
    else:
        keep[1 - odd] = before[0][1 - odd]
        send[1 - odd] = before[1][1 - odd]
    for kv in range(KVH):
        cols, vcols = cols_of(kv), cols_of(kv, KVW)
        keys, values = kall[:, cols], vall[:, cols]
        dv, dk = [], []
        for pair in range(REP // 2):
            at = slice(pair * 256, pair * 256 + 256)
            qs = jnp.concatenate([q[:, hc] for hc in heads_of(kv, pair)], 0)
            dos = jnp.concatenate([do[:, hc] for hc in heads_of(kv, pair)], 0)
            scores = dot_nt(keys, qs) * EXP2_SCALE + bias[...]
            top_own = stats[kv : kv + 1, at]
            top = jnp.maximum(jnp.max(scores, axis=0, keepdims=True), top_own)
            part = jnp.exp2(scores - top)
            shift = jnp.exp2(top_own - top)
            total = jnp.sum(part, axis=0, keepdims=True) + stats[4 + kv : 5 + kv, at] * shift
            inverse = 1.0 / total
            probs = part * inverse
            weights = probs.astype(BF16)
            factor = shift * inverse
            weights_own = (lifted[kv, :, at] * factor).astype(BF16)
            grad = dot_nt(values, dos)
            delta = jnp.sum(
                weights.astype(F32) * grad + weights_own.astype(F32) * pgrad[kv, :, at],
                axis=0, keepdims=True,
            )
            score = (probs * (grad - delta)).astype(BF16)
            ds[kv, :, at] = score
            rowstats[kv : kv + 1, at] = factor
            rowstats[4 + kv : 5 + kv, at] = delta
            dv.append((weights, dos))
            dk.append((score, qs))
        dv, dk = joined_dot(dv), joined_dot(dk)
        for out, old, part in ((keep, 0, slice(0, 64)), (send, 1, slice(64, 128))):
            for where, term in ((cols, dk[part]), (vcols, dv[part])):
                if slot:
                    term = term + before[old][odd, :, where]
                out[odd, :, where] = term


def grad_kernel(
    q0, do0, e0, g0, q1, do1, e1, g1, kown, ds0, row0, kall0, ds1, row1, kall1, after, dq, own
):
    slots = ((q0, do0, e0, g0, ds0, row0, kall0), (q1, do1, e1, g1, ds1, row1, kall1))
    for slot, (q, do, lifted, pgrad, ds, rowstats, kall) in enumerate(slots):
        rows = slice(slot * CLEN, (slot + 1) * CLEN)
        for kv in range(KVH):
            cols, vcols = cols_of(kv), cols_of(kv, KVW)
            keys = jnp.concatenate([kall[:, cols], kown[rows, cols]], 0)
            dv, dk = [], []
            for pair in range(REP // 2):
                at = slice(pair * 256, pair * 256 + 256)
                heads = heads_of(kv, pair)
                qs = jnp.concatenate([q[:, hc] for hc in heads], 0)
                dos = jnp.concatenate([do[:, hc] for hc in heads], 0)
                probs = lifted[kv, :, at] * rowstats[kv : kv + 1, at]
                delta = rowstats[4 + kv : 5 + kv, at]
                score = (probs * (pgrad[kv, :, at] - delta)).astype(BF16)
                dv.append((probs.astype(BF16), dos))
                dk.append((score, qs))
                scores = jnp.concatenate([ds[kv, :, at], score], 0)
                for j, hc in enumerate(heads):
                    dq[rows, hc] = dot_tn(scores[:, j * HD : (j + 1) * HD], keys)
            own[rows, cols] = joined_dot(dk)
            own[rows, vcols] = joined_dot(dv)


def scale_kernel(total, dq, own, after, query_grad, comp_key_grad, comp_value_grad, buf, kbuf, vbuf, sems):
    weight = ROWS / total[0:1, 0:1]
    scaled = weight * SCALE
    copies = []
    for i in range(KVH):
        cols = slice(i * QW, (i + 1) * QW)
        buf[:, cols] = (dq[:, cols] * scaled).astype(BF16)
        at = pl.ds(i * QW, QW)
        copies.append(pltpu.make_async_copy(buf.at[:, at], query_grad.at[:, at], sems.at[i]))
        copies[-1].start()
    kbuf[...] = (own[:, :KVW] * scaled).astype(BF16)
    vbuf[...] = (own[:, KVW:] * weight).astype(BF16)
    copies.append(pltpu.make_async_copy(kbuf, comp_key_grad, sems.at[4]))
    copies.append(pltpu.make_async_copy(vbuf, comp_value_grad, sems.at[5]))
    copies[-2].start()
    copies[-1].start()
    for copy in copies:
        copy.wait()


def chip_kernel(keep, got, k0, s1, s2, s3):
    for parity in range(2):
        both = keep[parity] + got[parity]
        k0[parity] = both[0:16]
        for m, out in enumerate((s1, s2, s3)):
            out[parity] = both[16 * (m + 1) : 16 * (m + 2)].astype(BF16)


def sum_kernel(near, far, k0, r1, r2, r3, after, also, k1, s1, s2, s3):
    y, _, _ = position()
    members = note_rows((near, far), 1) + note_rows((near, far), 2)
    for m, out in enumerate((k1, s1, s2, s3)):
        plane = y ^ m
        used = members[0] == plane.astype(F32)
        for member in members[1:]:
            used = used | (member == plane.astype(F32))
        used = jnp.broadcast_to(jnp.where(used, 1.0, 0.0), (16, HD))
        used = jnp.concatenate([used] * (2 * KVW // HD), 1)
        parity = plane & 1
        both = k0[parity]
        for ref in (r1, r2, r3):
            both += ref[parity].astype(F32)
        out[...] = (both * used).astype(out.dtype)


def last_kernel(total, k1, r1, r2, r3, dpk, dpv):
    weight = ROWS / total[0:1, 0:1]
    both = k1[...] + r1[...].astype(F32) + r2[...].astype(F32) + r3[...].astype(F32)
    dpk[...] = (both[:, :KVW] * (weight * SCALE)).astype(BF16)
    dpv[...] = (both[:, KVW:] * weight).astype(BF16)


SPECS = {
    "s": pl.BlockSpec(memory_space=pltpu.SMEM),
    "v": pl.BlockSpec(memory_space=VMEM),
    "a": pl.BlockSpec(memory_space=pl.ANY),
    "h": pl.BlockSpec(memory_space=pltpu.HBM),
}


def call(kernel, places, args, outs, out_places=None, scratch=(), limit=8):
    args = [
        pltpu.with_memory_space_constraint(x, pltpu.HBM) if p == "h" else x
        for p, x in zip(places, args, strict=True)
    ]
    return pl.pallas_call(
        kernel,
        out_shape=[jax.ShapeDtypeStruct(s, d) for s, d in outs],
        in_specs=[SPECS[p] for p in places],
        out_specs=[SPECS[p] for p in out_places or "v" * len(outs)],
        scratch_shapes=scratch,
        compiler_params=pltpu.CompilerParams(vmem_limit_bytes=limit * 2**20),
        cost_estimate=pl.CostEstimate(flops=1, bytes_accessed=1, transcendentals=0),
    )(*args)


def tie(x, after):
    return pl.pallas_call(
        tie_kernel,
        out_shape=jax.ShapeDtypeStruct(x.shape, x.dtype),
        in_specs=[SPECS["v"]] + [SPECS["a"]] * len(after),
        out_specs=SPECS["v"],
        input_output_aliases={0: 0},
        compiler_params=pltpu.CompilerParams(vmem_limit_bytes=2**20),
        cost_estimate=pl.CostEstimate(flops=1, bytes_accessed=1, transcendentals=0),
    )(x, *after)


def own_part(slot, comp_len, query, grad, kown, vown, after):
    def kernel(*refs):
        own_kernel(slot, *refs)

    return call(
        kernel, "hhhhha", [comp_len, query, grad, kown, vown, after],
        [
            ((CLEN, KVH * QW), BF16), ((CLEN, KVH * QW), BF16),
            ((KVH, CLEN, QW), F32), ((KVH, CLEN, QW), F32), ((8, QW), F32),
        ],
        scratch=[
            pltpu.SMEM((COMP,), jnp.int32), VMEM((CLEN, KVW), BF16), VMEM((CLEN, KVW), BF16),
            pltpu.SemaphoreType.DMA((11,)),
        ],
        limit=4
    )


def prompt_part(slot, group, prompt_len, parts, near, far, after, before=()):
    def kernel(*refs):
        prompt_kernel(slot, *refs)

    return call(
        kernel, "ss" + "v" * 13 + "a" + "v" * len(before),
        [group, prompt_len, *parts, *near, *far, after, *before],
        [
            ((KVH, PLEN, QW), BF16), ((8, QW), F32), ((PLEN, KVW), BF16),
            ((2, 64, 2 * KVW), F32), ((2, 64, 2 * KVW), F32),
        ],
        scratch=[VMEM((PLEN, KVW), BF16), VMEM((PLEN, 2 * CLEN), F32)],
        limit=4,
    )


def grad_part(parts0, parts1, kown, scores0, scores1, after):
    return call(
        grad_kernel, "v" * 15 + "a",
        [*parts0[:4], *parts1[:4], kown, *scores0, *scores1, after],
        [((COMP * CLEN, KVH * QW), F32), ((COMP * CLEN, 2 * KVW), F32)],
        limit=4,
    )


def scale_part(total, dq, own, after):
    rows = COMP * CLEN
    return call(
        scale_kernel, "vvva", [total, dq, own, after],
        [((rows, KVH * QW), BF16), ((rows, KVW), BF16), ((rows, KVW), BF16)], "hhh",
        scratch=[
            VMEM((rows, KVH * QW), BF16), VMEM((rows, KVW), BF16), VMEM((rows, KVW), BF16),
            pltpu.SemaphoreType.DMA((6,)),
        ],
        limit=8
    )


def swap(x, mask, axis="seq"):
    return lax.ppermute(x, axis, [(i, i ^ mask) for i in range(lax.axis_size(axis))])


def on_device(
    query, comp_key, comp_value, out_grad, prompt_key, prompt_value,
    prompt_len, comp_len, comp_group,
):
    wide = 2 * KVW
    (mine,) = call(
        pack_kernel, "hhhh", [comp_len, comp_group, prompt_key, prompt_value],
        [((16, wide + HD), BF16)],
        scratch=[
            pltpu.SMEM((COMP,), jnp.int32), pltpu.SMEM((COMP,), jnp.int32),
            pltpu.SemaphoreType.DMA((4,)),
        ],
    )
    chunks = [mine] + [swap(mine, 2 * m) for m in (1, 2, 3)]
    parts0 = own_part(0, comp_len, query, out_grad, comp_key, comp_value, mine)
    (plane,) = call(plane_kernel, "vvvva", [*chunks, parts0[4]], [((64, wide + HD), BF16)])
    near = [plane] + [swap(plane, 8 * m) for m in (1, 2, 3)]
    parts1 = own_part(1, comp_len, query, out_grad, comp_key, comp_value, plane)
    near[1] = tie(near[1], [parts1[4]])
    far = [swap(x, 1) for x in near]
    (count,) = call(count_kernel, "v" * 8, [*near, *far], [((8, HD), F32)])

    count1 = swap(count, 1, "grp")
    *scores0, keep, send = prompt_part(
        0, comp_group, prompt_len, parts0, near, far, count
    )
    count = count + count1
    *scores1, keep, send = prompt_part(
        1, comp_group, prompt_len, parts1, near, far, count, [keep, send]
    )
    got = swap(send, 1)
    k0, s1, s2, s3 = call(
        chip_kernel, "vv", [keep, got],
        [((2, 16, wide), F32)] + [((2, 16, wide), BF16)] * 3,
    )
    got = [swap(s, 2 * (m + 1)) for m, s in enumerate((s1, s2, s3))]
    dq, own = grad_part(parts0, parts1, comp_key, scores0, scores1, k0)
    count = count + swap(tie(count, [k0]), 2, "grp")
    k1, s1, s2, s3 = call(
        sum_kernel, "vvvvvvaa", [near[0], far[0], k0, *got, own, count],
        [((16, wide), F32)] + [((16, wide), BF16)] * 3,
    )
    got = [swap(s, 8 * (m + 1)) for m, s in enumerate((s1, s2, s3))]
    count = count + swap(tie(count, [k1]), 4, "grp")
    query_grad, comp_key_grad, comp_value_grad = scale_part(count, dq, own, k1)
    prompt_key_grad, prompt_value_grad = call(
        last_kernel, "vvvvv", [count, k1, *got], [((16, KVW), BF16)] * 2
    )
    return query_grad, comp_key_grad, comp_value_grad, prompt_key_grad, prompt_value_grad


def solution(mesh):
    rows, both = P(("grp", "seq"), None), P(("grp", "seq"))
    return jax.shard_map(
        on_device,
        mesh=mesh,
        in_specs=(rows,) * 6 + (P("grp"), both, both),
        out_specs=(rows,) * 5,
        check_vma=False,
    )
```

```python
import math

import jax
import jax.numpy as jnp
from jax import lax
from jax.experimental import pallas as pl
from jax.experimental.pallas import tpu as pltpu
from jax.sharding import PartitionSpec as P

HD = 128
CLEN = 128
PLEN = 128
COMP = 2
KVH = 4
REP = 8
KVW = KVH * HD
QW = REP * HD
GPR = 4
ROWS = 65536.0
SCALE = HD ** -0.5
EXP2_SCALE = SCALE * math.log2(math.e)
MASKED = -1e30
VMEM = pltpu.VMEM
F32 = jnp.float32
BF16 = jnp.bfloat16


def dot_nt(a, b):
    return lax.dot_general(a, b, (((1,), (1,)), ((), ())), preferred_element_type=F32)


def dot_nn(a, b):
    return lax.dot_general(a, b, (((1,), (0,)), ((), ())), preferred_element_type=F32)


def dot_tn(a, b):
    return lax.dot_general(a, b, (((0,), (0,)), ((), ())), preferred_element_type=F32)


def joined_dot(pairs):
    return dot_nn(
        jnp.concatenate([a for a, _ in pairs], 1), jnp.concatenate([b for _, b in pairs], 0)
    )


def position():
    place = lax.axis_index("seq")
    return place // 8, (place // 2) % 4, place % 2


def cols_of(kv, first=0):
    return slice(first + kv * HD, first + (kv + 1) * HD)


def heads_of(kv, pair):
    return [slice((kv * REP + 2 * pair + j) * HD, (kv * REP + 2 * pair + j + 1) * HD) for j in range(2)]


def pack_kernel(comp_len, comp_group, prompt_key, prompt_value, mine, lens, groups, sems):
    copies = [
        pltpu.make_async_copy(comp_len, lens, sems.at[0]),
        pltpu.make_async_copy(comp_group, groups, sems.at[1]),
        pltpu.make_async_copy(prompt_key, mine.at[:, pl.ds(0, KVW)], sems.at[2]),
        pltpu.make_async_copy(prompt_value, mine.at[:, pl.ds(KVW, KVW)], sems.at[3]),
    ]
    for copy in copies:
        copy.start()
    copies[0].wait()
    copies[1].wait()
    row = lax.broadcasted_iota(jnp.int32, (16, HD), 0)
    note = jnp.where(row == 0, lens[0] + lens[1], jnp.where(row == 1, groups[0], groups[1]))
    mine[:, 2 * KVW :] = note.astype(F32).astype(BF16)
    copies[2].wait()
    copies[3].wait()


def note_rows(refs, line):
    out = []
    for ref in refs:
        for part in range(4):
            block = ref[16 * part : 16 * part + 16, 2 * KVW :].astype(F32)
            out.append(block[line : line + 1])
    return out


def tie_kernel(*refs):
    pass


def plane_kernel(c0, c1, c2, c3, after, plane):
    for m, ref in enumerate((c0, c1, c2, c3)):
        plane[16 * m : 16 * m + 16, :] = ref[...]


def count_kernel(o0, o1, o2, o3, t0, t1, t2, t3, count):
    total = sum(note_rows((o0, o1, o2, o3, t0, t1, t2, t3), 0))
    count[...] = jnp.broadcast_to(total, count.shape)


def own_kernel(slot, comp_len, query, grad, kown, vown, after, q, do, lifted, pgrad, stats, lens, kbuf, vbuf, sems):
    rows = pl.ds(slot * CLEN, CLEN)
    small = [
        pltpu.make_async_copy(kown.at[rows], kbuf, sems.at[0]),
        pltpu.make_async_copy(vown.at[rows], vbuf, sems.at[1]),
        pltpu.make_async_copy(comp_len, lens, sems.at[10]),
    ]
    for copy in small:
        copy.start()
    copies = []
    for kv in range(KVH):
        cols = pl.ds(kv * QW, QW)
        copies.append(
            [
                pltpu.make_async_copy(query.at[rows, cols], q.at[:, cols], sems.at[2 + 2 * kv]),
                pltpu.make_async_copy(grad.at[rows, cols], do.at[:, cols], sems.at[3 + 2 * kv]),
            ]
        )
        for copy in copies[-1]:
            copy.start()
    row = lax.broadcasted_iota(jnp.int32, (CLEN, CLEN), 0)
    lane = lax.broadcasted_iota(jnp.int32, (CLEN, CLEN), 1)
    bias = jnp.where(row <= lane, 0.0, MASKED)
    bias = jnp.concatenate([bias, bias], 1)
    for copy in small:
        copy.wait()
    mask = jnp.where(row < lens[slot], 1.0, 0.0).astype(BF16)
    for kv in range(KVH):
        for copy in copies[kv]:
            copy.wait()
        keys = kbuf[:, cols_of(kv)]
        values = vbuf[:, cols_of(kv)]
        for pair in range(REP // 2):
            at = slice(pair * 256, pair * 256 + 256)
            dos = []
            for cols in heads_of(kv, pair):
                live = do[:, cols] * mask
                do[:, cols] = live
                dos.append(live)
            qs = jnp.concatenate([q[:, cols] for cols in heads_of(kv, pair)], 0)
            scores = dot_nt(keys, qs) * EXP2_SCALE + bias
            top = jnp.max(scores, axis=0, keepdims=True)
            part = jnp.exp2(scores - top)
            lifted[kv, :, at] = part
            stats[kv : kv + 1, at] = top
            stats[4 + kv : 5 + kv, at] = jnp.sum(part, axis=0, keepdims=True)
            pgrad[kv, :, at] = dot_nt(values, jnp.concatenate(dos, 0))


def prompt_kernel(
    group, prompt_len, q0, do0, e0, g0, st0, q1, do1, e1, g1, st1,
    o0, o1, o2, o3, t0, t1, t2, t3, after,
    ds0, row0, kall0, ds1, row1, kall1, keep, send, vall, bias,
):
    keep[...] = jnp.zeros_like(keep)
    send[...] = jnp.zeros_like(send)
    near, far = (o0, o1, o2, o3), (t0, t1, t2, t3)
    slots = ((q0, do0, e0, g0, st0, ds0, row0, kall0), (q1, do1, e1, g1, st1, ds1, row1, kall1))
    for slot, refs in enumerate(slots):
        prompt_slot(slot, group, prompt_len, near, far, *refs, keep, send, vall.at[slot], bias.at[slot])


def prompt_slot(
    slot, group, prompt_len, near, far, q, do, lifted, pgrad, stats, ds, rowstats, kall, keep, send, vall, bias
):
    y, z, c = position()
    row = lax.broadcasted_iota(jnp.int32, (PLEN, CLEN), 0)
    chunk = (((row // 16) % 4) ^ z) * 2 + ((row // 64) ^ c)
    place = chunk * 16 + row % 16
    for m in range(GPR):
        @pl.when((group[slot] ^ y) == m)
        def _():
            kall[0:64, :] = near[m][:, :KVW]
            kall[64:128, :] = far[m][:, :KVW]
            vall[0:64, :] = near[m][:, KVW : 2 * KVW]
            vall[64:128, :] = far[m][:, KVW : 2 * KVW]
    half = jnp.where(place < prompt_len[group[slot]], 0.0, MASKED)
    bias[...] = jnp.concatenate([half, half], 1)
    odd = group[slot] & 1
    for kvs in ((0, 1), (2, 3)):
        terms = {kv: ([], []) for kv in kvs}
        for pair in range(REP // 2):
            for kv in kvs:
                dv, dk = terms[kv]
                cols = cols_of(kv)
                keys, values = kall[:, cols], vall[:, cols]
                at = slice(pair * 256, pair * 256 + 256)
                qs = jnp.concatenate([q[:, hc] for hc in heads_of(kv, pair)], 0)
                dos = jnp.concatenate([do[:, hc] for hc in heads_of(kv, pair)], 0)
                scores = dot_nt(keys, qs) * EXP2_SCALE + bias[...]
                top_own = stats[kv : kv + 1, at]
                top = jnp.maximum(jnp.max(scores, axis=0, keepdims=True), top_own)
                part = jnp.exp2(scores - top)
                shift = jnp.exp2(top_own - top)
                total = jnp.sum(part, axis=0, keepdims=True) + stats[4 + kv : 5 + kv, at] * shift
                inverse = 1.0 / total
                probs = part * inverse
                weights = probs.astype(BF16)
                factor = shift * inverse
                weights_own = (lifted[kv, :, at] * factor).astype(BF16)
                grad = dot_nt(values, dos)
                delta = jnp.sum(
                    weights.astype(F32) * grad + weights_own.astype(F32) * pgrad[kv, :, at],
                    axis=0, keepdims=True,
                )
                score = (probs * (grad - delta)).astype(BF16)
                ds[kv, :, at] = score
                rowstats[kv : kv + 1, at] = factor
                rowstats[4 + kv : 5 + kv, at] = delta
                dv.append((weights, dos))
                dk.append((score, qs))
        for kv in kvs:
            cols, vcols = cols_of(kv), cols_of(kv, KVW)
            dv, dk = (joined_dot(t) for t in terms[kv])
            for out, part in ((keep, slice(0, 64)), (send, slice(64, 128))):
                out[odd, :, cols] += dk[part]
                out[odd, :, vcols] += dv[part]


def grad_kernel(
    q0, do0, e0, g0, q1, do1, e1, g1, kown, ds0, row0, kall0, ds1, row1, kall1, after, dq, own
):
    slots = ((q0, do0, e0, g0, ds0, row0, kall0), (q1, do1, e1, g1, ds1, row1, kall1))
    for slot, (q, do, lifted, pgrad, ds, rowstats, kall) in enumerate(slots):
        rows = slice(slot * CLEN, (slot + 1) * CLEN)
        for kv in range(KVH):
            cols, vcols = cols_of(kv), cols_of(kv, KVW)
            keys = jnp.concatenate([kall[:, cols], kown[rows, cols]], 0)
            dv, dk = [], []
            for pair in range(REP // 2):
                at = slice(pair * 256, pair * 256 + 256)
                heads = heads_of(kv, pair)
                qs = jnp.concatenate([q[:, hc] for hc in heads], 0)
                dos = jnp.concatenate([do[:, hc] for hc in heads], 0)
                probs = lifted[kv, :, at] * rowstats[kv : kv + 1, at]
                delta = rowstats[4 + kv : 5 + kv, at]
                score = (probs * (pgrad[kv, :, at] - delta)).astype(BF16)
                dv.append((probs.astype(BF16), dos))
                dk.append((score, qs))
                scores = jnp.concatenate([ds[kv, :, at], score], 0)
                for j, hc in enumerate(heads):
                    dq[rows, hc] = dot_tn(scores[:, j * HD : (j + 1) * HD], keys)
            own[rows, cols] = joined_dot(dk)
            own[rows, vcols] = joined_dot(dv)


def scale_kernel(total, dq, own, after, query_grad, comp_key_grad, comp_value_grad, buf, kbuf, vbuf, sems):
    weight = ROWS / total[0:1, 0:1]
    scaled = weight * SCALE
    copies = []
    for i in range(KVH):
        cols = slice(i * QW, (i + 1) * QW)
        buf[:, cols] = (dq[:, cols] * scaled).astype(BF16)
        at = pl.ds(i * QW, QW)
        copies.append(pltpu.make_async_copy(buf.at[:, at], query_grad.at[:, at], sems.at[i]))
        copies[-1].start()
    kbuf[...] = (own[:, :KVW] * scaled).astype(BF16)
    vbuf[...] = (own[:, KVW:] * weight).astype(BF16)
    copies.append(pltpu.make_async_copy(kbuf, comp_key_grad, sems.at[4]))
    copies.append(pltpu.make_async_copy(vbuf, comp_value_grad, sems.at[5]))
    copies[-2].start()
    copies[-1].start()
    for copy in copies:
        copy.wait()


def chip_kernel(keep, got, k0, s1, s2, s3):
    for parity in range(2):
        both = keep[parity] + got[parity]
        k0[parity] = both[0:16]
        for m, out in enumerate((s1, s2, s3)):
            out[parity] = both[16 * (m + 1) : 16 * (m + 2)].astype(BF16)


def sum_kernel(near, far, k0, r1, r2, r3, after, also, k1, s1, s2, s3):
    y, _, _ = position()
    members = note_rows((near, far), 1) + note_rows((near, far), 2)
    for m, out in enumerate((k1, s1, s2, s3)):
        plane = y ^ m
        used = members[0] == plane.astype(F32)
        for member in members[1:]:
            used = used | (member == plane.astype(F32))
        used = jnp.broadcast_to(jnp.where(used, 1.0, 0.0), (16, HD))
        used = jnp.concatenate([used] * (2 * KVW // HD), 1)
        parity = plane & 1
        both = k0[parity]
        for ref in (r1, r2, r3):
            both += ref[parity].astype(F32)
        out[...] = (both * used).astype(out.dtype)


def last_kernel(total, k1, r1, r2, r3, dpk, dpv):
    weight = ROWS / total[0:1, 0:1]
    both = k1[...] + r1[...].astype(F32) + r2[...].astype(F32) + r3[...].astype(F32)
    dpk[...] = (both[:, :KVW] * (weight * SCALE)).astype(BF16)
    dpv[...] = (both[:, KVW:] * weight).astype(BF16)


SPECS = {
    "s": pl.BlockSpec(memory_space=pltpu.SMEM),
    "v": pl.BlockSpec(memory_space=VMEM),
    "a": pl.BlockSpec(memory_space=pl.ANY),
    "h": pl.BlockSpec(memory_space=pltpu.HBM),
}


def call(kernel, places, args, outs, out_places=None, scratch=(), limit=8):
    args = [
        pltpu.with_memory_space_constraint(x, pltpu.HBM) if p == "h" else x
        for p, x in zip(places, args, strict=True)
    ]
    return pl.pallas_call(
        kernel,
        out_shape=[jax.ShapeDtypeStruct(s, d) for s, d in outs],
        in_specs=[SPECS[p] for p in places],
        out_specs=[SPECS[p] for p in out_places or "v" * len(outs)],
        scratch_shapes=scratch,
        compiler_params=pltpu.CompilerParams(vmem_limit_bytes=limit * 2**20),
        cost_estimate=pl.CostEstimate(flops=1, bytes_accessed=1, transcendentals=0),
    )(*args)


def tie(x, after):
    return pl.pallas_call(
        tie_kernel,
        out_shape=jax.ShapeDtypeStruct(x.shape, x.dtype),
        in_specs=[SPECS["v"]] + [SPECS["a"]] * len(after),
        out_specs=SPECS["v"],
        input_output_aliases={0: 0},
        compiler_params=pltpu.CompilerParams(vmem_limit_bytes=2**20),
        cost_estimate=pl.CostEstimate(flops=1, bytes_accessed=1, transcendentals=0),
    )(x, *after)


def own_part(slot, comp_len, query, grad, kown, vown, after):
    def kernel(*refs):
        own_kernel(slot, *refs)

    return call(
        kernel, "hhhhha", [comp_len, query, grad, kown, vown, after],
        [
            ((CLEN, KVH * QW), BF16), ((CLEN, KVH * QW), BF16),
            ((KVH, CLEN, QW), F32), ((KVH, CLEN, QW), F32), ((8, QW), F32),
        ],
        scratch=[
            pltpu.SMEM((COMP,), jnp.int32), VMEM((CLEN, KVW), BF16), VMEM((CLEN, KVW), BF16),
            pltpu.SemaphoreType.DMA((11,)),
        ],
        limit=4
    )


def prompt_part(group, prompt_len, parts0, parts1, near, far, after):
    scores = [((KVH, PLEN, QW), BF16), ((8, QW), F32), ((PLEN, KVW), BF16)]
    outs = call(
        prompt_kernel, "ss" + "v" * 18 + "a",
        [group, prompt_len, *parts0, *parts1, *near, *far, after],
        scores * 2 + [((2, 64, 2 * KVW), F32)] * 2,
        scratch=[VMEM((COMP, PLEN, KVW), BF16), VMEM((COMP, PLEN, 2 * CLEN), F32)],
        limit=4,
    )
    return outs[:3], outs[3:6], outs[6], outs[7]


def grad_part(parts0, parts1, kown, scores0, scores1, after):
    return call(
        grad_kernel, "v" * 15 + "a",
        [*parts0[:4], *parts1[:4], kown, *scores0, *scores1, after],
        [((COMP * CLEN, KVH * QW), F32), ((COMP * CLEN, 2 * KVW), F32)],
        limit=4,
    )


def scale_part(total, dq, own, after):
    rows = COMP * CLEN
    return call(
        scale_kernel, "vvva", [total, dq, own, after],
        [((rows, KVH * QW), BF16), ((rows, KVW), BF16), ((rows, KVW), BF16)], "hhh",
        scratch=[
            VMEM((rows, KVH * QW), BF16), VMEM((rows, KVW), BF16), VMEM((rows, KVW), BF16),
            pltpu.SemaphoreType.DMA((6,)),
        ],
        limit=8
    )


def swap(x, mask, axis="seq"):
    return lax.ppermute(x, axis, [(i, i ^ mask) for i in range(lax.axis_size(axis))])


def on_device(
    query, comp_key, comp_value, out_grad, prompt_key, prompt_value,
    prompt_len, comp_len, comp_group,
):
    wide = 2 * KVW
    (mine,) = call(
        pack_kernel, "hhhh", [comp_len, comp_group, prompt_key, prompt_value],
        [((16, wide + HD), BF16)],
        scratch=[
            pltpu.SMEM((COMP,), jnp.int32), pltpu.SMEM((COMP,), jnp.int32),
            pltpu.SemaphoreType.DMA((4,)),
        ],
    )
    chunks = [mine] + [swap(mine, 2 * m) for m in (1, 2, 3)]
    parts0 = own_part(0, comp_len, query, out_grad, comp_key, comp_value, mine)
    (plane,) = call(plane_kernel, "vvvva", [*chunks, parts0[4]], [((64, wide + HD), BF16)])
    near = [plane] + [swap(plane, 8 * m) for m in (1, 2, 3)]
    parts1 = own_part(1, comp_len, query, out_grad, comp_key, comp_value, plane)
    near[1] = tie(near[1], [parts1[4]])
    far = [swap(x, 1) for x in near]
    (count,) = call(count_kernel, "v" * 8, [*near, *far], [((8, HD), F32)])

    counts = [swap(count, 2 * m, "grp") for m in (1, 2, 3)]
    scores0, scores1, keep, send = prompt_part(
        comp_group, prompt_len, parts0, parts1, near, far, count
    )
    count = sum(counts, count)
    got = swap(tie(send, [count]), 1)
    k0, s1, s2, s3 = call(
        chip_kernel, "vv", [keep, got],
        [((2, 16, wide), F32)] + [((2, 16, wide), BF16)] * 3,
    )
    got = [swap(s, 2 * (m + 1)) for m, s in enumerate((s1, s2, s3))]
    dq, own = grad_part(parts0, parts1, comp_key, scores0, scores1, k0)
    count = tie(count, [k0])
    count = count + swap(count, 1, "grp")
    k1, s1, s2, s3 = call(
        sum_kernel, "vvvvvvaa", [near[0], far[0], k0, *got, own, count],
        [((16, wide), F32)] + [((16, wide), BF16)] * 3,
    )
    got = [swap(s, 8 * (m + 1)) for m, s in enumerate((s1, s2, s3))]
    query_grad, comp_key_grad, comp_value_grad = scale_part(count, dq, own, k1)
    prompt_key_grad, prompt_value_grad = call(
        last_kernel, "vvvvv", [count, k1, *got], [((16, KVW), BF16)] * 2
    )
    return query_grad, comp_key_grad, comp_value_grad, prompt_key_grad, prompt_value_grad


def solution(mesh):
    rows, both = P(("grp", "seq"), None), P(("grp", "seq"))
    return jax.shard_map(
        on_device,
        mesh=mesh,
        in_specs=(rows,) * 6 + (P("grp"), both, both),
        out_specs=(rows,) * 5,
        check_vma=False,
    )
```

```python
import math

import jax
import jax.numpy as jnp
from jax import lax
from jax.experimental import pallas as pl
from jax.experimental.pallas import tpu as pltpu
from jax.sharding import PartitionSpec as P

HD = 128
CLEN = 128
PLEN = 128
COMP = 2
KVH = 4
REP = 8
KVW = KVH * HD
QW = REP * HD
GPR = 4
ROWS = 65536.0
SCALE = HD ** -0.5
EXP2_SCALE = SCALE * math.log2(math.e)
MASKED = -1e30
VMEM = pltpu.VMEM
F32 = jnp.float32
BF16 = jnp.bfloat16


def dot_nt(a, b):
    return lax.dot_general(a, b, (((1,), (1,)), ((), ())), preferred_element_type=F32)


def dot_nn(a, b):
    return lax.dot_general(a, b, (((1,), (0,)), ((), ())), preferred_element_type=F32)


def dot_tn(a, b):
    return lax.dot_general(a, b, (((0,), (0,)), ((), ())), preferred_element_type=F32)


def joined_dot(pairs):
    return dot_nn(
        jnp.concatenate([a for a, _ in pairs], 1), jnp.concatenate([b for _, b in pairs], 0)
    )


def position():
    place = lax.axis_index("seq")
    return place // 8, (place // 2) % 4, place % 2


def cols_of(kv, first=0):
    return slice(first + kv * HD, first + (kv + 1) * HD)


def heads_of(kv, pair):
    return [slice((kv * REP + 2 * pair + j) * HD, (kv * REP + 2 * pair + j + 1) * HD) for j in range(2)]


def pack_kernel(comp_len, comp_group, prompt_key, prompt_value, mine, lens, groups, sems):
    copies = [
        pltpu.make_async_copy(comp_len, lens, sems.at[0]),
        pltpu.make_async_copy(comp_group, groups, sems.at[1]),
        pltpu.make_async_copy(prompt_key, mine.at[:, pl.ds(0, KVW)], sems.at[2]),
        pltpu.make_async_copy(prompt_value, mine.at[:, pl.ds(KVW, KVW)], sems.at[3]),
    ]
    for copy in copies:
        copy.start()
    copies[0].wait()
    copies[1].wait()
    row = lax.broadcasted_iota(jnp.int32, (16, HD), 0)
    note = jnp.where(row == 0, lens[0] + lens[1], jnp.where(row == 1, groups[0], groups[1]))
    mine[:, 2 * KVW :] = note.astype(F32).astype(BF16)
    copies[2].wait()
    copies[3].wait()


def note_rows(refs, line):
    out = []
    for ref in refs:
        for part in range(4):
            block = ref[16 * part : 16 * part + 16, 2 * KVW :].astype(F32)
            out.append(block[line : line + 1])
    return out


def tie_kernel(*refs):
    pass


def plane_kernel(c0, c1, c2, c3, after, plane):
    for m, ref in enumerate((c0, c1, c2, c3)):
        plane[16 * m : 16 * m + 16, :] = ref[...]


def count_kernel(o0, o1, o2, o3, t0, t1, t2, t3, count):
    total = sum(note_rows((o0, o1, o2, o3, t0, t1, t2, t3), 0))
    count[...] = jnp.broadcast_to(total, count.shape)


def own_kernel(slot, comp_len, query, grad, kown, vown, after, q, do, lifted, pgrad, stats, lens, kbuf, vbuf, sems):
    rows = pl.ds(slot * CLEN, CLEN)
    small = [
        pltpu.make_async_copy(kown.at[rows], kbuf, sems.at[0]),
        pltpu.make_async_copy(vown.at[rows], vbuf, sems.at[1]),
        pltpu.make_async_copy(comp_len, lens, sems.at[10]),
    ]
    for copy in small:
        copy.start()
    copies = []
    for kv in range(KVH):
        cols = pl.ds(kv * QW, QW)
        copies.append(
            [
                pltpu.make_async_copy(query.at[rows, cols], q.at[:, cols], sems.at[2 + 2 * kv]),
                pltpu.make_async_copy(grad.at[rows, cols], do.at[:, cols], sems.at[3 + 2 * kv]),
            ]
        )
        for copy in copies[-1]:
            copy.start()
    row = lax.broadcasted_iota(jnp.int32, (CLEN, CLEN), 0)
    lane = lax.broadcasted_iota(jnp.int32, (CLEN, CLEN), 1)
    bias = jnp.where(row <= lane, 0.0, MASKED)
    bias = jnp.concatenate([bias, bias], 1)
    for copy in small:
        copy.wait()
    mask = jnp.where(row < lens[slot], 1.0, 0.0).astype(BF16)
    for kv in range(KVH):
        for copy in copies[kv]:
            copy.wait()
        keys = kbuf[:, cols_of(kv)]
        values = vbuf[:, cols_of(kv)]
        for pair in range(REP // 2):
            at = slice(pair * 256, pair * 256 + 256)
            dos = []
            for cols in heads_of(kv, pair):
                live = do[:, cols] * mask
                do[:, cols] = live
                dos.append(live)
            qs = jnp.concatenate([q[:, cols] for cols in heads_of(kv, pair)], 0)
            scores = dot_nt(keys, qs) * EXP2_SCALE + bias
            top = jnp.max(scores, axis=0, keepdims=True)
            part = jnp.exp2(scores - top)
            lifted[kv, :, at] = part
            stats[kv : kv + 1, at] = top
            stats[4 + kv : 5 + kv, at] = jnp.sum(part, axis=0, keepdims=True)
            pgrad[kv, :, at] = dot_nt(values, jnp.concatenate(dos, 0))


def prompt_kernel(
    group, prompt_len, q0, do0, e0, g0, st0, q1, do1, e1, g1, st1,
    o0, o1, o2, o3, t0, t1, t2, t3, after,
    ds0, row0, kall0, ds1, row1, kall1, keep, send, vall, bias,
):
    keep[...] = jnp.zeros_like(keep)
    send[...] = jnp.zeros_like(send)
    near, far = (o0, o1, o2, o3), (t0, t1, t2, t3)
    slots = ((q0, do0, e0, g0, st0, ds0, row0, kall0), (q1, do1, e1, g1, st1, ds1, row1, kall1))
    for slot, refs in enumerate(slots):
        prompt_slot(slot, group, prompt_len, near, far, *refs, keep, send, vall.at[slot], bias.at[slot])


def prompt_slot(
    slot, group, prompt_len, near, far, q, do, lifted, pgrad, stats, ds, rowstats, kall, keep, send, vall, bias
):
    y, z, c = position()
    row = lax.broadcasted_iota(jnp.int32, (PLEN, CLEN), 0)
    chunk = (((row // 16) % 4) ^ z) * 2 + ((row // 64) ^ c)
    place = chunk * 16 + row % 16
    for m in range(GPR):
        @pl.when((group[slot] ^ y) == m)
        def _():
            kall[0:64, :] = near[m][:, :KVW]
            kall[64:128, :] = far[m][:, :KVW]
            vall[0:64, :] = near[m][:, KVW : 2 * KVW]
            vall[64:128, :] = far[m][:, KVW : 2 * KVW]
    half = jnp.where(place < prompt_len[group[slot]], 0.0, MASKED)
    bias[...] = jnp.concatenate([half, half], 1)
    odd = group[slot] & 1
    for kvs in ((0, 1), (2, 3)):
        terms = {kv: ([], []) for kv in kvs}
        for pair in range(REP // 2):
            for kv in kvs:
                dv, dk = terms[kv]
                cols = cols_of(kv)
                keys, values = kall[:, cols], vall[:, cols]
                at = slice(pair * 256, pair * 256 + 256)
                qs = jnp.concatenate([q[:, hc] for hc in heads_of(kv, pair)], 0)
                dos = jnp.concatenate([do[:, hc] for hc in heads_of(kv, pair)], 0)
                scores = dot_nt(keys, qs) * EXP2_SCALE + bias[...]
                top_own = stats[kv : kv + 1, at]
                top = jnp.maximum(jnp.max(scores, axis=0, keepdims=True), top_own)
                part = jnp.exp2(scores - top)
                shift = jnp.exp2(top_own - top)
                total = jnp.sum(part, axis=0, keepdims=True) + stats[4 + kv : 5 + kv, at] * shift
                inverse = 1.0 / total
                probs = part * inverse
                weights = probs.astype(BF16)
                factor = shift * inverse
                weights_own = (lifted[kv, :, at] * factor).astype(BF16)
                grad = dot_nt(values, dos)
                delta = jnp.sum(
                    weights.astype(F32) * grad + weights_own.astype(F32) * pgrad[kv, :, at],
                    axis=0, keepdims=True,
                )
                score = (probs * (grad - delta)).astype(BF16)
                ds[kv, :, at] = score
                rowstats[kv : kv + 1, at] = factor
                rowstats[4 + kv : 5 + kv, at] = delta
                dv.append((weights, dos))
                dk.append((score, qs))
        for kv in kvs:
            cols, vcols = cols_of(kv), cols_of(kv, KVW)
            dv, dk = (joined_dot(t) for t in terms[kv])
            for out, part in ((keep, slice(0, 64)), (send, slice(64, 128))):
                out[odd, :, cols] += dk[part]
                out[odd, :, vcols] += dv[part]


def grad_kernel(
    q0, do0, e0, g0, q1, do1, e1, g1, kown, ds0, row0, kall0, ds1, row1, kall1, after, dq, own
):
    slots = ((q0, do0, e0, g0, ds0, row0, kall0), (q1, do1, e1, g1, ds1, row1, kall1))
    for slot, (q, do, lifted, pgrad, ds, rowstats, kall) in enumerate(slots):
        rows = slice(slot * CLEN, (slot + 1) * CLEN)
        for kv in range(KVH):
            cols, vcols = cols_of(kv), cols_of(kv, KVW)
            keys = jnp.concatenate([kall[:, cols], kown[rows, cols]], 0)
            dv, dk = [], []
            for pair in range(REP // 2):
                at = slice(pair * 256, pair * 256 + 256)
                heads = heads_of(kv, pair)
                qs = jnp.concatenate([q[:, hc] for hc in heads], 0)
                dos = jnp.concatenate([do[:, hc] for hc in heads], 0)
                probs = lifted[kv, :, at] * rowstats[kv : kv + 1, at]
                delta = rowstats[4 + kv : 5 + kv, at]
                score = (probs * (pgrad[kv, :, at] - delta)).astype(BF16)
                dv.append((probs.astype(BF16), dos))
                dk.append((score, qs))
                scores = jnp.concatenate([ds[kv, :, at], score], 0)
                for j, hc in enumerate(heads):
                    dq[rows, hc] = dot_tn(scores[:, j * HD : (j + 1) * HD], keys)
            own[rows, cols] = joined_dot(dk)
            own[rows, vcols] = joined_dot(dv)


def scale_kernel(total, dq, own, after, query_grad, comp_key_grad, comp_value_grad, buf, kbuf, vbuf, sems):
    weight = ROWS / total[0:1, 0:1]
    scaled = weight * SCALE
    copies = []
    for i in range(KVH):
        cols = slice(i * QW, (i + 1) * QW)
        buf[:, cols] = (dq[:, cols] * scaled).astype(BF16)
        at = pl.ds(i * QW, QW)
        copies.append(pltpu.make_async_copy(buf.at[:, at], query_grad.at[:, at], sems.at[i]))
        copies[-1].start()
    kbuf[...] = (own[:, :KVW] * scaled).astype(BF16)
    vbuf[...] = (own[:, KVW:] * weight).astype(BF16)
    copies.append(pltpu.make_async_copy(kbuf, comp_key_grad, sems.at[4]))
    copies.append(pltpu.make_async_copy(vbuf, comp_value_grad, sems.at[5]))
    copies[-2].start()
    copies[-1].start()
    for copy in copies:
        copy.wait()


def chip_kernel(keep, got, k0, s1, s2, s3):
    for parity in range(2):
        both = keep[parity] + got[parity]
        k0[parity] = both[0:16]
        for m, out in enumerate((s1, s2, s3)):
            out[parity] = both[16 * (m + 1) : 16 * (m + 2)].astype(BF16)


def sum_kernel(near, far, k0, r1, r2, r3, after, also, k1, s1, s2, s3):
    y, _, _ = position()
    members = note_rows((near, far), 1) + note_rows((near, far), 2)
    for m, out in enumerate((k1, s1, s2, s3)):
        plane = y ^ m
        used = members[0] == plane.astype(F32)
        for member in members[1:]:
            used = used | (member == plane.astype(F32))
        used = jnp.broadcast_to(jnp.where(used, 1.0, 0.0), (16, HD))
        used = jnp.concatenate([used] * (2 * KVW // HD), 1)
        parity = plane & 1
        both = k0[parity]
        for ref in (r1, r2, r3):
            both += ref[parity].astype(F32)
        out[...] = (both * used).astype(out.dtype)


def last_kernel(total, k1, r1, r2, r3, dpk, dpv):
    weight = ROWS / total[0:1, 0:1]
    both = k1[...] + r1[...].astype(F32) + r2[...].astype(F32) + r3[...].astype(F32)
    dpk[...] = (both[:, :KVW] * (weight * SCALE)).astype(BF16)
    dpv[...] = (both[:, KVW:] * weight).astype(BF16)


SPECS = {
    "s": pl.BlockSpec(memory_space=pltpu.SMEM),
    "v": pl.BlockSpec(memory_space=VMEM),
    "a": pl.BlockSpec(memory_space=pl.ANY),
    "h": pl.BlockSpec(memory_space=pltpu.HBM),
}


def call(kernel, places, args, outs, out_places=None, scratch=(), limit=8):
    args = [
        pltpu.with_memory_space_constraint(x, pltpu.HBM) if p == "h" else x
        for p, x in zip(places, args, strict=True)
    ]
    return pl.pallas_call(
        kernel,
        out_shape=[jax.ShapeDtypeStruct(s, d) for s, d in outs],
        in_specs=[SPECS[p] for p in places],
        out_specs=[SPECS[p] for p in out_places or "v" * len(outs)],
        scratch_shapes=scratch,
        compiler_params=pltpu.CompilerParams(vmem_limit_bytes=limit * 2**20),
        cost_estimate=pl.CostEstimate(flops=1, bytes_accessed=1, transcendentals=0),
    )(*args)


def tie(x, after):
    return pl.pallas_call(
        tie_kernel,
        out_shape=jax.ShapeDtypeStruct(x.shape, x.dtype),
        in_specs=[SPECS["v"]] + [SPECS["a"]] * len(after),
        out_specs=SPECS["v"],
        input_output_aliases={0: 0},
        compiler_params=pltpu.CompilerParams(vmem_limit_bytes=2**20),
        cost_estimate=pl.CostEstimate(flops=1, bytes_accessed=1, transcendentals=0),
    )(x, *after)


def own_part(slot, comp_len, query, grad, kown, vown, after):
    def kernel(*refs):
        own_kernel(slot, *refs)

    return call(
        kernel, "hhhhha", [comp_len, query, grad, kown, vown, after],
        [
            ((CLEN, KVH * QW), BF16), ((CLEN, KVH * QW), BF16),
            ((KVH, CLEN, QW), F32), ((KVH, CLEN, QW), F32), ((8, QW), F32),
        ],
        scratch=[
            pltpu.SMEM((COMP,), jnp.int32), VMEM((CLEN, KVW), BF16), VMEM((CLEN, KVW), BF16),
            pltpu.SemaphoreType.DMA((11,)),
        ],
        limit=4
    )


def prompt_part(group, prompt_len, parts0, parts1, near, far, after):
    scores = [((KVH, PLEN, QW), BF16), ((8, QW), F32), ((PLEN, KVW), BF16)]
    outs = call(
        prompt_kernel, "ss" + "v" * 18 + "a",
        [group, prompt_len, *parts0, *parts1, *near, *far, after],
        scores * 2 + [((2, 64, 2 * KVW), F32)] * 2,
        scratch=[VMEM((COMP, PLEN, KVW), BF16), VMEM((COMP, PLEN, 2 * CLEN), F32)],
        limit=4,
    )
    return outs[:3], outs[3:6], outs[6], outs[7]


def grad_part(parts0, parts1, kown, scores0, scores1, after):
    return call(
        grad_kernel, "v" * 15 + "a",
        [*parts0[:4], *parts1[:4], kown, *scores0, *scores1, after],
        [((COMP * CLEN, KVH * QW), F32), ((COMP * CLEN, 2 * KVW), F32)],
        limit=4,
    )


def scale_part(total, dq, own, after):
    rows = COMP * CLEN
    return call(
        scale_kernel, "vvva", [total, dq, own, after],
        [((rows, KVH * QW), BF16), ((rows, KVW), BF16), ((rows, KVW), BF16)], "hhh",
        scratch=[
            VMEM((rows, KVH * QW), BF16), VMEM((rows, KVW), BF16), VMEM((rows, KVW), BF16),
            pltpu.SemaphoreType.DMA((6,)),
        ],
        limit=8
    )


def swap(x, mask, axis="seq"):
    return lax.ppermute(x, axis, [(i, i ^ mask) for i in range(lax.axis_size(axis))])


def on_device(
    query, comp_key, comp_value, out_grad, prompt_key, prompt_value,
    prompt_len, comp_len, comp_group,
):
    wide = 2 * KVW
    (mine,) = call(
        pack_kernel, "hhhh", [comp_len, comp_group, prompt_key, prompt_value],
        [((16, wide + HD), BF16)],
        scratch=[
            pltpu.SMEM((COMP,), jnp.int32), pltpu.SMEM((COMP,), jnp.int32),
            pltpu.SemaphoreType.DMA((4,)),
        ],
    )
    chunks = [mine] + [swap(mine, 2 * m) for m in (1, 2, 3)]
    parts0 = own_part(0, comp_len, query, out_grad, comp_key, comp_value, mine)
    (plane,) = call(plane_kernel, "vvvva", [*chunks, parts0[4]], [((64, wide + HD), BF16)])
    near = [plane] + [swap(plane, 8 * m) for m in (1, 2, 3)]
    parts1 = own_part(1, comp_len, query, out_grad, comp_key, comp_value, plane)
    near[1] = tie(near[1], [parts1[4]])
    far = [swap(x, 1) for x in near]
    (count,) = call(count_kernel, "v" * 8, [*near, *far], [((8, HD), F32)])

    counts = [swap(count, 2 * m, "grp") for m in (1, 2, 3)]
    scores0, scores1, keep, send = prompt_part(
        comp_group, prompt_len, parts0, parts1, near, far, count
    )
    count = sum(counts, count)
    got = swap(tie(send, [count]), 1)
    k0, s1, s2, s3 = call(
        chip_kernel, "vv", [keep, got],
        [((2, 16, wide), F32)] + [((2, 16, wide), BF16)] * 3,
    )
    got = [swap(s, 2 * m) for m, s in ((3, s3), (2, s2), (1, s1))]
    dq, own = grad_part(parts0, parts1, comp_key, scores0, scores1, k0)
    count = tie(count, [k0])
    count = count + swap(count, 1, "grp")
    k1, s1, s2, s3 = call(
        sum_kernel, "vvvvvvaa", [near[0], far[0], k0, *got, own, count],
        [((16, wide), F32)] + [((16, wide), BF16)] * 3,
    )
    got = [swap(s, 8 * m) for m, s in ((2, s2), (3, s3), (1, s1))]
    query_grad, comp_key_grad, comp_value_grad = scale_part(count, dq, own, k1)
    prompt_key_grad, prompt_value_grad = call(
        last_kernel, "vvvvv", [count, k1, *got], [((16, KVW), BF16)] * 2
    )
    return query_grad, comp_key_grad, comp_value_grad, prompt_key_grad, prompt_value_grad


def solution(mesh):
    rows, both = P(("grp", "seq"), None), P(("grp", "seq"))
    return jax.shard_map(
        on_device,
        mesh=mesh,
        in_specs=(rows,) * 6 + (P("grp"), both, both),
        out_specs=(rows,) * 5,
        check_vma=False,
    )
```

```python
import math

import jax
import jax.numpy as jnp
from jax import lax
from jax.experimental import pallas as pl
from jax.experimental.pallas import tpu as pltpu
from jax.sharding import PartitionSpec as P

HD = 128
CLEN = 128
PLEN = 128
COMP = 2
KVH = 4
REP = 8
KVW = KVH * HD
QW = REP * HD
GPR = 4
ROWS = 65536.0
SCALE = HD ** -0.5
EXP2_SCALE = SCALE * math.log2(math.e)
MASKED = -1e30
VMEM = pltpu.VMEM
F32 = jnp.float32
BF16 = jnp.bfloat16


def dot_nt(a, b):
    return lax.dot_general(a, b, (((1,), (1,)), ((), ())), preferred_element_type=F32)


def dot_nn(a, b):
    return lax.dot_general(a, b, (((1,), (0,)), ((), ())), preferred_element_type=F32)


def dot_tn(a, b):
    return lax.dot_general(a, b, (((0,), (0,)), ((), ())), preferred_element_type=F32)


def joined_dot(pairs):
    return dot_nn(
        jnp.concatenate([a for a, _ in pairs], 1), jnp.concatenate([b for _, b in pairs], 0)
    )


def position():
    place = lax.axis_index("seq")
    return place // 8, (place // 2) % 4, place % 2


def cols_of(kv, first=0):
    return slice(first + kv * HD, first + (kv + 1) * HD)


def heads_of(kv, pair):
    return [slice((kv * REP + 2 * pair + j) * HD, (kv * REP + 2 * pair + j + 1) * HD) for j in range(2)]


def pack_kernel(comp_len, comp_group, prompt_key, prompt_value, mine, lens, groups, sems):
    copies = [
        pltpu.make_async_copy(comp_len, lens, sems.at[0]),
        pltpu.make_async_copy(comp_group, groups, sems.at[1]),
        pltpu.make_async_copy(prompt_key, mine.at[:, pl.ds(0, KVW)], sems.at[2]),
        pltpu.make_async_copy(prompt_value, mine.at[:, pl.ds(KVW, KVW)], sems.at[3]),
    ]
    for copy in copies:
        copy.start()
    copies[0].wait()
    copies[1].wait()
    row = lax.broadcasted_iota(jnp.int32, (16, HD), 0)
    note = jnp.where(row == 0, lens[0] + lens[1], jnp.where(row == 1, groups[0], groups[1]))
    mine[:, 2 * KVW :] = note.astype(F32).astype(BF16)
    copies[2].wait()
    copies[3].wait()


def note_rows(refs, line):
    out = []
    for ref in refs:
        for part in range(4):
            block = ref[16 * part : 16 * part + 16, 2 * KVW :].astype(F32)
            out.append(block[line : line + 1])
    return out


def tie_kernel(*refs):
    pass


def plane_kernel(c0, c1, c2, c3, after, plane):
    for m, ref in enumerate((c0, c1, c2, c3)):
        plane[16 * m : 16 * m + 16, :] = ref[...]


def count_kernel(o0, o1, o2, o3, t0, t1, t2, t3, count):
    total = sum(note_rows((o0, o1, o2, o3, t0, t1, t2, t3), 0))
    count[...] = jnp.broadcast_to(total, count.shape)


def own_kernel(slot, comp_len, query, grad, kown, vown, after, q, do, lifted, pgrad, stats, lens, kbuf, vbuf, sems):
    rows = pl.ds(slot * CLEN, CLEN)
    small = [
        pltpu.make_async_copy(kown.at[rows], kbuf, sems.at[0]),
        pltpu.make_async_copy(vown.at[rows], vbuf, sems.at[1]),
        pltpu.make_async_copy(comp_len, lens, sems.at[10]),
    ]
    for copy in small:
        copy.start()
    copies = []
    for kv in range(KVH):
        cols = pl.ds(kv * QW, QW)
        copies.append(
            [
                pltpu.make_async_copy(query.at[rows, cols], q.at[:, cols], sems.at[2 + 2 * kv]),
                pltpu.make_async_copy(grad.at[rows, cols], do.at[:, cols], sems.at[3 + 2 * kv]),
            ]
        )
        for copy in copies[-1]:
            copy.start()
    row = lax.broadcasted_iota(jnp.int32, (CLEN, CLEN), 0)
    lane = lax.broadcasted_iota(jnp.int32, (CLEN, CLEN), 1)
    bias = jnp.where(row <= lane, 0.0, MASKED)
    bias = jnp.concatenate([bias, bias], 1)
    for copy in small:
        copy.wait()
    mask = jnp.where(row < lens[slot], 1.0, 0.0).astype(BF16)
    for kv in range(KVH):
        for copy in copies[kv]:
            copy.wait()
        keys = kbuf[:, cols_of(kv)]
        values = vbuf[:, cols_of(kv)]
        for pair in range(REP // 2):
            at = slice(pair * 256, pair * 256 + 256)
            dos = []
            for cols in heads_of(kv, pair):
                live = do[:, cols] * mask
                do[:, cols] = live
                dos.append(live)
            qs = jnp.concatenate([q[:, cols] for cols in heads_of(kv, pair)], 0)
            scores = dot_nt(keys, qs) * EXP2_SCALE + bias
            top = jnp.max(scores, axis=0, keepdims=True)
            part = jnp.exp2(scores - top)
            lifted[kv, :, at] = part
            stats[kv : kv + 1, at] = top
            stats[4 + kv : 5 + kv, at] = jnp.sum(part, axis=0, keepdims=True)
            pgrad[kv, :, at] = dot_nt(values, jnp.concatenate(dos, 0))


def prompt_kernel(
    group, prompt_len, q0, do0, e0, g0, st0, q1, do1, e1, g1, st1,
    o0, o1, o2, o3, t0, t1, t2, t3, after,
    ds0, row0, kall0, ds1, row1, kall1, keep, send, vall, bias,
):
    keep[...] = jnp.zeros_like(keep)
    send[...] = jnp.zeros_like(send)
    near, far = (o0, o1, o2, o3), (t0, t1, t2, t3)
    slots = ((q0, do0, e0, g0, st0, ds0, row0, kall0), (q1, do1, e1, g1, st1, ds1, row1, kall1))
    for slot, refs in enumerate(slots):
        prompt_slot(slot, group, prompt_len, near, far, *refs, keep, send, vall.at[slot], bias.at[slot])


def prompt_slot(
    slot, group, prompt_len, near, far, q, do, lifted, pgrad, stats, ds, rowstats, kall, keep, send, vall, bias
):
    y, z, c = position()
    row = lax.broadcasted_iota(jnp.int32, (PLEN, CLEN), 0)
    chunk = (((row // 16) % 4) ^ z) * 2 + ((row // 64) ^ c)
    place = chunk * 16 + row % 16
    for m in range(GPR):
        @pl.when((group[slot] ^ y) == m)
        def _():
            kall[0:64, :] = near[m][:, :KVW]
            kall[64:128, :] = far[m][:, :KVW]
            vall[0:64, :] = near[m][:, KVW : 2 * KVW]
            vall[64:128, :] = far[m][:, KVW : 2 * KVW]
    half = jnp.where(place < prompt_len[group[slot]], 0.0, MASKED)
    bias[...] = jnp.concatenate([half, half], 1)
    odd = group[slot] & 1
    for kvs in ((0, 1), (2, 3)):
        terms = {kv: ([], []) for kv in kvs}
        for pair in range(REP // 2):
            for kv in kvs:
                dv, dk = terms[kv]
                cols = cols_of(kv)
                keys, values = kall[:, cols], vall[:, cols]
                at = slice(pair * 256, pair * 256 + 256)
                qs = jnp.concatenate([q[:, hc] for hc in heads_of(kv, pair)], 0)
                dos = jnp.concatenate([do[:, hc] for hc in heads_of(kv, pair)], 0)
                scores = dot_nt(keys, qs) * EXP2_SCALE + bias[...]
                top_own = stats[kv : kv + 1, at]
                top = jnp.maximum(jnp.max(scores, axis=0, keepdims=True), top_own)
                part = jnp.exp2(scores - top)
                shift = jnp.exp2(top_own - top)
                total = jnp.sum(part, axis=0, keepdims=True) + stats[4 + kv : 5 + kv, at] * shift
                inverse = 1.0 / total
                probs = part * inverse
                weights = probs.astype(BF16)
                factor = shift * inverse
                weights_own = (lifted[kv, :, at] * factor).astype(BF16)
                grad = dot_nt(values, dos)
                delta = jnp.sum(
                    weights.astype(F32) * grad + weights_own.astype(F32) * pgrad[kv, :, at],
                    axis=0, keepdims=True,
                )
                score = (probs * (grad - delta)).astype(BF16)
                ds[kv, :, at] = score
                rowstats[kv : kv + 1, at] = factor
                rowstats[4 + kv : 5 + kv, at] = delta
                dv.append((weights, dos))
                dk.append((score, qs))
        for kv in kvs:
            cols, vcols = cols_of(kv), cols_of(kv, KVW)
            dv, dk = (joined_dot(t) for t in terms[kv])
            for out, part in ((keep, slice(0, 64)), (send, slice(64, 128))):
                out[odd, :, cols] += dk[part]
                out[odd, :, vcols] += dv[part]


def grad_kernel(
    q0, do0, e0, g0, q1, do1, e1, g1, kown, ds0, row0, kall0, ds1, row1, kall1, after, dq, own
):
    slots = ((q0, do0, e0, g0, ds0, row0, kall0), (q1, do1, e1, g1, ds1, row1, kall1))
    for slot, (q, do, lifted, pgrad, ds, rowstats, kall) in enumerate(slots):
        rows = slice(slot * CLEN, (slot + 1) * CLEN)
        for kv in range(KVH):
            cols, vcols = cols_of(kv), cols_of(kv, KVW)
            keys = jnp.concatenate([kall[:, cols], kown[rows, cols]], 0)
            dv, dk = [], []
            for pair in range(REP // 2):
                at = slice(pair * 256, pair * 256 + 256)
                heads = heads_of(kv, pair)
                qs = jnp.concatenate([q[:, hc] for hc in heads], 0)
                dos = jnp.concatenate([do[:, hc] for hc in heads], 0)
                probs = lifted[kv, :, at] * rowstats[kv : kv + 1, at]
                delta = rowstats[4 + kv : 5 + kv, at]
                score = (probs * (pgrad[kv, :, at] - delta)).astype(BF16)
                dv.append((probs.astype(BF16), dos))
                dk.append((score, qs))
                scores = jnp.concatenate([ds[kv, :, at], score], 0)
                for j, hc in enumerate(heads):
                    dq[rows, hc] = dot_tn(scores[:, j * HD : (j + 1) * HD], keys)
            own[rows, cols] = joined_dot(dk)
            own[rows, vcols] = joined_dot(dv)


def scale_kernel(total, dq, own, after, query_grad, comp_key_grad, comp_value_grad, buf, kbuf, vbuf, sems):
    weight = ROWS / total[0:1, 0:1]
    scaled = weight * SCALE
    copies = []
    for i in range(KVH):
        cols = slice(i * QW, (i + 1) * QW)
        buf[:, cols] = (dq[:, cols] * scaled).astype(BF16)
        at = pl.ds(i * QW, QW)
        copies.append(pltpu.make_async_copy(buf.at[:, at], query_grad.at[:, at], sems.at[i]))
        copies[-1].start()
    kbuf[...] = (own[:, :KVW] * scaled).astype(BF16)
    vbuf[...] = (own[:, KVW:] * weight).astype(BF16)
    copies.append(pltpu.make_async_copy(kbuf, comp_key_grad, sems.at[4]))
    copies.append(pltpu.make_async_copy(vbuf, comp_value_grad, sems.at[5]))
    copies[-2].start()
    copies[-1].start()
    for copy in copies:
        copy.wait()


def chip_kernel(keep, got, k0, s1, s2, s3):
    for parity in range(2):
        both = keep[parity] + got[parity]
        k0[parity] = both[0:16]
        for m, out in enumerate((s1, s2, s3)):
            out[parity] = both[16 * (m + 1) : 16 * (m + 2)].astype(BF16)


def sum_kernel(near, far, k0, r1, r2, r3, after, also, k1, s1, s2, s3):
    y, _, _ = position()
    members = note_rows((near, far), 1) + note_rows((near, far), 2)
    for m, out in enumerate((k1, s1, s2, s3)):
        plane = y ^ m
        used = members[0] == plane.astype(F32)
        for member in members[1:]:
            used = used | (member == plane.astype(F32))
        used = jnp.broadcast_to(jnp.where(used, 1.0, 0.0), (16, HD))
        used = jnp.concatenate([used] * (2 * KVW // HD), 1)
        parity = plane & 1
        both = k0[parity]
        for ref in (r1, r2, r3):
            both += ref[parity].astype(F32)
        out[...] = (both * used).astype(out.dtype)


def last_kernel(total, k1, r1, r2, r3, dpk, dpv):
    weight = ROWS / total[0:1, 0:1]
    both = k1[...] + r1[...].astype(F32) + r2[...].astype(F32) + r3[...].astype(F32)
    dpk[...] = (both[:, :KVW] * (weight * SCALE)).astype(BF16)
    dpv[...] = (both[:, KVW:] * weight).astype(BF16)


SPECS = {
    "s": pl.BlockSpec(memory_space=pltpu.SMEM),
    "v": pl.BlockSpec(memory_space=VMEM),
    "a": pl.BlockSpec(memory_space=pl.ANY),
    "h": pl.BlockSpec(memory_space=pltpu.HBM),
}


def call(kernel, places, args, outs, out_places=None, scratch=(), limit=8):
    args = [
        pltpu.with_memory_space_constraint(x, pltpu.HBM) if p == "h" else x
        for p, x in zip(places, args, strict=True)
    ]
    return pl.pallas_call(
        kernel,
        out_shape=[jax.ShapeDtypeStruct(s, d) for s, d in outs],
        in_specs=[SPECS[p] for p in places],
        out_specs=[SPECS[p] for p in out_places or "v" * len(outs)],
        scratch_shapes=scratch,
        compiler_params=pltpu.CompilerParams(vmem_limit_bytes=limit * 2**20),
        cost_estimate=pl.CostEstimate(flops=1, bytes_accessed=1, transcendentals=0),
    )(*args)


def tie(x, after):
    return pl.pallas_call(
        tie_kernel,
        out_shape=jax.ShapeDtypeStruct(x.shape, x.dtype),
        in_specs=[SPECS["v"]] + [SPECS["a"]] * len(after),
        out_specs=SPECS["v"],
        input_output_aliases={0: 0},
        compiler_params=pltpu.CompilerParams(vmem_limit_bytes=2**20),
        cost_estimate=pl.CostEstimate(flops=1, bytes_accessed=1, transcendentals=0),
    )(x, *after)


def own_part(slot, comp_len, query, grad, kown, vown, after):
    def kernel(*refs):
        own_kernel(slot, *refs)

    return call(
        kernel, "hhhhha", [comp_len, query, grad, kown, vown, after],
        [
            ((CLEN, KVH * QW), BF16), ((CLEN, KVH * QW), BF16),
            ((KVH, CLEN, QW), F32), ((KVH, CLEN, QW), F32), ((8, QW), F32),
        ],
        scratch=[
            pltpu.SMEM((COMP,), jnp.int32), VMEM((CLEN, KVW), BF16), VMEM((CLEN, KVW), BF16),
            pltpu.SemaphoreType.DMA((11,)),
        ],
        limit=4
    )


def prompt_part(group, prompt_len, parts0, parts1, near, far, after):
    scores = [((KVH, PLEN, QW), BF16), ((8, QW), F32), ((PLEN, KVW), BF16)]
    outs = call(
        prompt_kernel, "ss" + "v" * 18 + "a",
        [group, prompt_len, *parts0, *parts1, *near, *far, after],
        scores * 2 + [((2, 64, 2 * KVW), F32)] * 2,
        scratch=[VMEM((COMP, PLEN, KVW), BF16), VMEM((COMP, PLEN, 2 * CLEN), F32)],
        limit=4,
    )
    return outs[:3], outs[3:6], outs[6], outs[7]


def grad_part(parts0, parts1, kown, scores0, scores1, after):
    return call(
        grad_kernel, "v" * 15 + "a",
        [*parts0[:4], *parts1[:4], kown, *scores0, *scores1, after],
        [((COMP * CLEN, KVH * QW), F32), ((COMP * CLEN, 2 * KVW), F32)],
        limit=4,
    )


def scale_part(total, dq, own, after):
    rows = COMP * CLEN
    return call(
        scale_kernel, "vvva", [total, dq, own, after],
        [((rows, KVH * QW), BF16), ((rows, KVW), BF16), ((rows, KVW), BF16)], "hhh",
        scratch=[
            VMEM((rows, KVH * QW), BF16), VMEM((rows, KVW), BF16), VMEM((rows, KVW), BF16),
            pltpu.SemaphoreType.DMA((6,)),
        ],
        limit=8
    )


def swap(x, mask, axis="seq"):
    return lax.ppermute(x, axis, [(i, i ^ mask) for i in range(lax.axis_size(axis))])


def on_device(
    query, comp_key, comp_value, out_grad, prompt_key, prompt_value,
    prompt_len, comp_len, comp_group,
):
    wide = 2 * KVW
    (mine,) = call(
        pack_kernel, "hhhh", [comp_len, comp_group, prompt_key, prompt_value],
        [((16, wide + HD), BF16)],
        scratch=[
            pltpu.SMEM((COMP,), jnp.int32), pltpu.SMEM((COMP,), jnp.int32),
            pltpu.SemaphoreType.DMA((4,)),
        ],
    )
    chunks = [mine] + [swap(mine, 2 * m) for m in (1, 2, 3)]
    parts0 = own_part(0, comp_len, query, out_grad, comp_key, comp_value, mine)
    (plane,) = call(plane_kernel, "vvvva", [*chunks, parts0[4]], [((64, wide + HD), BF16)])
    near = [plane] + [swap(plane, 8 * m) for m in (1, 2, 3)]
    parts1 = own_part(1, comp_len, query, out_grad, comp_key, comp_value, plane)
    near[1] = tie(near[1], [parts1[4]])
    far = [swap(x, 1) for x in near]
    (count,) = call(count_kernel, "v" * 8, [*near, *far], [((8, HD), F32)])

    counts = [swap(count, 2 * m, "grp") for m in (1, 2, 3)]
    scores0, scores1, keep, send = prompt_part(
        comp_group, prompt_len, parts0, parts1, near, far, count
    )
    count = sum(counts, count)
    got = swap(tie(send, [count]), 1)
    k0, s1, s2, s3 = call(
        chip_kernel, "vv", [keep, got],
        [((2, 16, wide), F32)] + [((2, 16, wide), BF16)] * 3,
    )
    got = [swap(s, 2 * m) for m, s in ((3, s3), (2, s2), (1, s1))]
    dq, own = grad_part(parts0, parts1, comp_key, scores0, scores1, k0)
    count = tie(count, [k0])
    count = count + swap(count, 1, "grp")
    k1, s1, s2, s3 = call(
        sum_kernel, "vvvvvvaa", [near[0], far[0], k0, *got, own, count],
        [((16, wide), F32)] + [((16, wide), BF16)] * 3,
    )
    got = [swap(s, 8 * m) for m, s in ((3, s3), (2, s2), (1, s1))]
    query_grad, comp_key_grad, comp_value_grad = scale_part(count, dq, own, k1)
    prompt_key_grad, prompt_value_grad = call(
        last_kernel, "vvvvv", [count, k1, *got], [((16, KVW), BF16)] * 2
    )
    return query_grad, comp_key_grad, comp_value_grad, prompt_key_grad, prompt_value_grad


def solution(mesh):
    rows, both = P(("grp", "seq"), None), P(("grp", "seq"))
    return jax.shard_map(
        on_device,
        mesh=mesh,
        in_specs=(rows,) * 6 + (P("grp"), both, both),
        out_specs=(rows,) * 5,
        check_vma=False,
    )
```
